32 devices in a mesh: px: 8 (over z, x), py: 4 (over y, core).
Axes of the slice: x: 2, y: 2, z: 4, core: 2. Of those that a mesh axis runs over, the one named last changes fastest.
Arguments:
- start_field: float32 [512, 512, 256], P('px', 'py'), may hold values from 0.25 to 4
- end_adjoint: float32 [512, 512, 256], P('px', 'py'), may hold values from 0.25 to 4
- potential: float32 [512, 512, 256], P('px', 'py'), may hold values from -15 to 15
- line_xy: float32 [512, 512], replicated, may hold values from -1 to 2
- line_z: float32 [256, 256], replicated, may hold values from -1 to 2
Outputs:
- final_field: float32 [512, 512, 256], P('px', 'py')
- first_adjoint: float32 [512, 512, 256], P('px', 'py')
- density: float32 [512, 512, 256], P('px', 'py')
The draws below stay inside these ranges and needn't reach their ends.
All inputs are finite; a program needn't handle non-finite values.
Results may differ from the reference program's by a relative error of at most 0.0001.
Values sent between devices are 32-bit elements; how exact they have to be, the bound alone decides.
No kernel may reach another device: no remote copies, remote signals or barrier semaphores. Data moves between devices by JAX's collectives and lax.ppermute only.
A program may use at most 256 MiB of HBM per device.

```python
import math
import jax
import jax.numpy as jnp
from jax import lax

NX = 512
NZ = 256
STEPS = 1


def draw_line_xy(key, part):
    key = jax.random.fold_in(key, 11)
    rows = jnp.arange(NX)[:, None]
    columns = jnp.arange(NX)[None, :]
    identity = jnp.where(rows == columns, 1.0, 0.0).astype(jnp.float32)
    noise = jnp.clip(jax.random.normal(key, (NX, NX), jnp.float32), -3.0, 3.0)
    return identity + 0.5 / NX ** 0.5 * noise


def draw_line_z(key, part):
    key = jax.random.fold_in(key, 23)
    rows = jnp.arange(NZ)[:, None]
    columns = jnp.arange(NZ)[None, :]
    identity = jnp.where(rows == columns, 1.0, 0.0).astype(jnp.float32)
    noise = jnp.clip(jax.random.normal(key, (NZ, NZ), jnp.float32), -3.0, 3.0)
    return identity + 0.5 / NZ ** 0.5 * noise


def block_levels(key, shape, shards, low, largest):
    def one(position, shards_of):
        steps = jax.random.uniform(jax.random.fold_in(jax.random.fold_in(key, 6), position), (shards_of,), jnp.float32, low / len(shards), largest / len(shards))
        return jnp.repeat(jnp.exp(steps), shape[position] // shards_of).reshape((-1,) + (1,) * (len(shape) - position - 1))

    level = one(*shards[0])
    for cut in shards[1:]:
        level = level * one(*cut)
    return level


def bell_draw(stream_key, shape, deviation, bound, pieces=(), kind=jnp.bfloat16):
    factor_of = block_levels(stream_key, shape, pieces, -0.22, 0.18) if pieces else 1.0
    array = jax.random.normal(stream_key, shape, jnp.float32) * deviation * factor_of
    return jnp.minimum(jnp.maximum(array, -bound), bound).astype(kind)


def setup_inputs(seed: int = 0) -> dict:
    seeds = jax.random.split(jax.random.key(seed), 6)
    start_field = jnp.clip(jnp.exp(math.log(4.0) - 2.7725887 * jax.random.uniform(seeds[0], (NX, NX, NZ), jnp.float32) ** block_levels(seeds[0], (NX, NX, NZ), ((0, 8), (1, 4)), -0.2, 0.2)), 0.25, 4.0)
    end_adjoint = jnp.clip(jnp.exp(math.log(4.0) - 2.7725887 * jax.random.uniform(seeds[1], (NX, NX, NZ), jnp.float32) ** block_levels(seeds[1], (NX, NX, NZ), ((0, 8), (1, 4)), -0.2, 0.2)), 0.25, 4.0)
    potential = bell_draw(seeds[2], (NX, NX, NZ), 3.0, 15.0, ((0, 8), (1, 4)), jnp.float32)
    line_xy = draw_line_xy(jax.random.fold_in(seeds[5], 71), 0)
    line_z = draw_line_z(jax.random.fold_in(seeds[5], 71), 0)
    return {"start_field": start_field, "end_adjoint": end_adjoint, "potential": potential, "line_xy": line_xy, "line_z": line_z}


def along(field, matrix, axis):
    if axis == 0:
        return jnp.einsum('jbc,ij->ibc', field, matrix, precision=lax.Precision.HIGHEST)
    if axis == 1:
        return jnp.einsum('ajc,ij->aic', field, matrix, precision=lax.Precision.HIGHEST)
    return jnp.einsum('abj,ij->abi', field, matrix, precision=lax.Precision.HIGHEST)


def propagate(field, half, line_xy, line_z, adjoint):
    matrix_xy = line_xy.T if adjoint else line_xy
    matrix_z = line_z.T if adjoint else line_z
    moved = half * field
    moved = along(moved, matrix_z, 2)
    moved = along(moved, matrix_xy, 1)
    moved = along(moved, matrix_xy, 0)
    return half * moved


def reference(start_field, end_adjoint, potential, line_xy, line_z):
    half = jnp.exp(-0.05 * potential)
    forward_list = [start_field]
    for index in range(STEPS):
        forward_list.append(propagate(forward_list[-1], half, line_xy, line_z, False))
    adjoint_list = [end_adjoint]
    for index in range(STEPS):
        adjoint_list.append(propagate(adjoint_list[-1], half, line_xy, line_z, True))
    adjoint_list = adjoint_list[::-1]
    density = jnp.zeros_like(start_field)
    for index in range(STEPS + 1):
        weight = 0.5 if index == 0 or index == STEPS else 1.0
        density = density + (0.1 * weight) * forward_list[index] * adjoint_list[index]
    return forward_list[-1], adjoint_list[0], density
```

```python
import functools

import jax
import jax.numpy as jnp
from jax import lax
from jax.experimental import pallas as pl
from jax.experimental.pallas import tpu as pltpu
from jax.sharding import PartitionSpec as P

F32 = jnp.float32
ROWS = 8
LANES = 128
VMEM_LIMIT = 56 * 1024 * 1024


def product(left, right):
    return jnp.dot(left, right, precision=lax.Precision.HIGHEST, preferred_element_type=F32)


def two_parts(value):
    high = lax.reduce_precision(value, 8, 7)
    return [high.astype(jnp.bfloat16), (value - high).astype(jnp.bfloat16)]


def split_in_kernel(value):
    high = value.astype(jnp.bfloat16)
    return high, (value - high.astype(F32)).astype(jnp.bfloat16)


def dot(left, right):
    return jnp.dot(left, right, preferred_element_type=F32)


def lines_times(lines, matrix_refs):
    high, low = split_in_kernel(lines)
    matrix_high, matrix_low = matrix_refs[0][...], matrix_refs[1][...]
    return dot(high, matrix_high) + (dot(high, matrix_low) + dot(low, matrix_high))


def times_lines(matrix_refs, lines):
    high, low = split_in_kernel(lines)
    matrix_high, matrix_low = matrix_refs[0][...], matrix_refs[1][...]
    return dot(matrix_high, high) + (dot(matrix_low, high) + dot(matrix_high, low))


def half_of(potential):
    return jnp.exp(-0.05 * potential)


def call(kernel, name, grid, in_specs, out_specs, outs, scratch, flops, touched, aliases=None):
    return pl.pallas_call(
        kernel,
        name=name,
        grid=grid,
        in_specs=in_specs,
        out_specs=out_specs,
        out_shape=outs,
        scratch_shapes=scratch,
        input_output_aliases=aliases or {},
        cost_estimate=pl.CostEstimate(flops=flops, bytes_accessed=touched, transcendentals=0),
        compiler_params=pltpu.CompilerParams(vmem_limit_bytes=VMEM_LIMIT),
    )


def table_spec():
    return pl.BlockSpec(memory_space=pltpu.SMEM)


def whole_spec(shape):
    return pl.BlockSpec(shape, lambda i: (0,) * len(shape))


def to_of(me, r, n):
    pairs = n // 2
    return ((me // 2 + r // 2) % pairs) * 2 + (me % 2 + r % 2) % 2


def from_of(me, r, n):
    pairs = n // 2
    return ((me // 2 + pairs - r // 2) % pairs) * 2 + (me % 2 + r % 2) % 2


def after(value, *earlier):
    if isinstance(value, list):
        return [after(value[0], *earlier), *value[1:]]
    return lax.optimization_barrier((value, *earlier))[0] if earlier else value


class Flow:
    def __init__(self, depth, lag):
        self.depth, self.lag = depth, lag
        self.landed = {"px": [], "py": []}
        self.latest = []
        self.due = []

    def back(self, axis):
        landed, depth = self.landed[axis], self.depth[axis]
        return landed[max(0, len(landed) - 2 * depth + 1) : max(0, len(landed) - depth + 1)]

    def owe(self, kind, array):
        self.due.append((len(self.landed["px"]) + self.lag[kind], array))

    def work(self, function, s, value, *rest, back=True):
        out = function(s, after(value, *self.latest, *(self.back("px") if back else [])), *rest)
        self.latest = [jax.tree.leaves(out)[0]]
        if back:
            self.owe("work", self.latest[0])
        return out

    def settle(self, depth):
        self.due = [(0, array) for _, array in self.due] + [(0, array) for array in self.latest]
        self.depth["px"] = depth

    def permute(self, axis, block, pairs):
        count = len(self.landed["px"])
        if axis == "px":
            pins = self.back("px") + [array for when, array in self.due if when <= count]
            self.due = [(when, array) for when, array in self.due if when > count]
        else:
            pins = self.back("py") + self.back("px")[-1:]
        got = lax.ppermute(after(block, *pins), axis, pairs)
        self.landed[axis].append(got)
        if axis == "py":
            self.owe("py", got)
        return got


class Exchange:
    def __init__(self, flow, axis, blocks):
        self.flow, self.axis, self.blocks, self.n = flow, axis, blocks, len(blocks)
        self.got = [blocks[0]] + [None] * (self.n - 1)
        self.order = sorted(range(1, self.n), key=lambda r: (r % 2, abs(2 * (r // 2) - self.n // 2), r))
        self.left = list(self.order)

    def send(self, count):
        for r in self.left[:count]:
            pairs = [(device, to_of(device, r, self.n)) for device in range(self.n)]
            self.got[r] = self.flow.permute(self.axis, self.blocks[r], pairs)
        self.left = self.left[count:]
        return self

    def rest(self):
        return self.send(self.n).got


class Sizes:
    def __init__(self, field_shape, count_px, count_py):
        self.nx, self.ny = count_px, count_py
        self.a, self.b, self.c = field_shape
        self.full = self.a * count_px
        self.by = self.b // count_px
        self.ax = self.a // count_py
        self.yc = ROWS
        self.chunks = self.by // ROWS
        self.parts = [(k, slice(k * LANES, (k + 1) * LANES)) for k in range(self.c // LANES)]
        self.field_bytes = 4 * self.a * self.b * self.c


def turn_spec(s, part):
    return pl.BlockSpec((s.a, s.yc, LANES), lambda i: (0, 0, part))


def first_in(s, field, chunk, potential, z_turned, to_px):
    def kernel(to_ref, f_ref, w_ref, high_ref, low_ref, *rest):
        outs, held = rest[:-1], rest[-1]
        moved = half_of(w_ref[...]) * f_ref[...]
        moved = lines_times(moved.reshape(2 * ROWS * s.nx * s.yc, s.c), (high_ref, low_ref))
        held[...] = moved.reshape(2 * ROWS, s.nx, s.yc, s.c)
        for r, out in enumerate(outs):
            out[...] = held[:, to_ref[r]]

    block = pl.BlockSpec((2 * ROWS, s.nx, s.yc, s.c), lambda i: (i, 0, chunk, 0))
    out = pl.BlockSpec((2 * ROWS, s.yc, s.c), lambda i: (i, 0, 0))
    view = (s.a, s.nx, s.by, s.c)
    return call(
        kernel,
        "z_lines_by_px",
        (s.a // (2 * ROWS),),
        [table_spec(), block, block] + [whole_spec((s.c, s.c))] * 2,
        [out] * s.nx,
        [jax.ShapeDtypeStruct((s.a, s.yc, s.c), F32)] * s.nx,
        [pltpu.VMEM((2 * ROWS, s.nx, s.yc, s.c), F32)],
        6 * s.a * s.b * s.c * s.c // s.chunks,
        3 * s.field_bytes // s.chunks,
    )(to_px, field.reshape(view), potential.reshape(view), *z_turned)


def first_by_py(s, field, potential, z_turned, to_py):
    step = ROWS // 2

    def kernel(to_ref, f_ref, w_ref, high_ref, low_ref, *outs):
        for r in range(s.ny):
            q = to_ref[r]
            moved = half_of(w_ref[q]) * f_ref[q]
            moved = lines_times(moved.reshape(step * s.b, s.c), (high_ref, low_ref))
            outs[r][...] = moved.reshape(step, s.b, s.c)

    block = pl.BlockSpec((s.ny, step, s.b, s.c), lambda i: (0, i, 0, 0))
    out = pl.BlockSpec((step, s.b, s.c), lambda i: (i, 0, 0))
    view = (s.ny, s.ax, s.b, s.c)
    return call(
        kernel,
        "z_lines_by_py",
        (s.ax // step,),
        [table_spec(), block, block] + [whole_spec((s.c, s.c))] * 2,
        [out] * s.ny,
        [jax.ShapeDtypeStruct((s.ax, s.b, s.c), F32)] * s.ny,
        [],
        6 * s.a * s.b * s.c * s.c,
        3 * s.field_bytes,
    )(to_py, field.reshape(view), potential.reshape(view), *z_turned)


def x_lines_forward(s, got, matrix, from_px, to_px, to_py):
    def kernel(from_ref, to_ref, part_ref, high_ref, low_ref, *rest):
        count = len(s.parts) * s.nx
        ins, outs = rest[:count], rest[count:-2]
        lines, moved = rest[-2:]
        y = pl.program_id(0)
        for place in range(count):
            r, (_, lanes) = place // len(s.parts), s.parts[place % len(s.parts)]
            rows = ins[place].reshape(s.a * s.yc, LANES)
            lines[pl.ds(pl.multiple_of(from_ref[r] * s.a, s.a), s.a), lanes] = rows[pl.ds(y, s.a, stride=s.yc), :]
        moved[...] = times_lines((high_ref, low_ref), lines[...])
        for r in range(s.nx):
            for k in range(s.ny):
                at = pl.multiple_of(to_ref[r] * s.a + part_ref[k] * s.ax, s.ax)
                outs[r][k, 0] = moved[pl.ds(at, s.ax), :]

    parted = pl.BlockSpec((s.ny, 1, s.ax, s.c), lambda i: (0, i, 0, 0))
    return call(
        kernel,
        "x_lines_forward",
        (s.yc,),
        [table_spec()] * 3
        + [whole_spec((s.full, s.full))] * 2
        + [turn_spec(s, part) for _ in range(s.nx) for part, _ in s.parts],
        [parted] * s.nx,
        [jax.ShapeDtypeStruct((s.ny, s.yc, s.ax, s.c), F32)] * s.nx,
        [pltpu.VMEM((s.full, s.c), F32), pltpu.VMEM((s.full, s.c), F32)],
        6 * s.a * s.b * s.c * s.full // s.chunks,
        2 * s.field_bytes // s.chunks,
    )(from_px, to_px, to_py, *matrix, *[block for block in got for _ in s.parts])


def x_lines_adjoint(s, got, matrix, from_px, to_px, from_py):
    def kernel(from_ref, to_ref, part_ref, high_ref, low_ref, *rest):
        ins, outs = rest[: s.nx], rest[s.nx : -3]
        lines, moved, held = rest[-3:]
        y = pl.program_id(0)
        for r in range(s.nx):
            for k in range(s.ny):
                at = pl.multiple_of(from_ref[r] * s.a + part_ref[k] * s.ax, s.ax)
                lines[pl.ds(at, s.ax), :] = ins[r][k, 0]
        moved[...] = times_lines((high_ref, low_ref), lines[...])
        for r in range(s.nx):
            for part, lanes in s.parts:
                taken = moved[pl.ds(pl.multiple_of(to_ref[r] * s.a, s.a), s.a), lanes]
                held[part, r, pl.ds(y, s.a, stride=s.yc), :] = taken

        @pl.when(y == s.yc - 1)
        def _():
            for r in range(s.nx):
                for part, lanes in s.parts:
                    outs[r][:, :, lanes] = held[part, r].reshape(s.a, s.yc, LANES)

    parted = pl.BlockSpec((s.ny, 1, s.ax, s.c), lambda i: (0, i, 0, 0))
    return call(
        kernel,
        "x_lines_adjoint",
        (s.yc,),
        [table_spec()] * 3 + [whole_spec((s.full, s.full))] * 2 + [parted] * s.nx,
        [whole_spec((s.a, s.yc, s.c))] * s.nx,
        [jax.ShapeDtypeStruct((s.a, s.yc, s.c), F32)] * s.nx,
        [
            pltpu.VMEM((s.full, s.c), F32),
            pltpu.VMEM((s.full, s.c), F32),
            pltpu.VMEM((len(s.parts), s.nx, s.a * s.yc, LANES), F32),
        ],
        6 * s.a * s.b * s.c * s.full // s.chunks,
        2 * s.field_bytes // s.chunks,
    )(from_px, to_px, from_py, *matrix, *got)


def y_lines_unturned(s, got, matrix, from_px, from_py, to_py):
    def kernel(px_ref, from_ref, to_ref, high_ref, low_ref, *rest):
        count = len(s.parts) * s.chunks * s.ny
        ins, outs = rest[:count], rest[count:-2]
        lines, moved = rest[-2:]

        @pl.loop(0, ROWS)
        def _(x):
            for place in range(count):
                part, lanes = s.parts[place % len(s.parts)]
                k, chunk = place // len(s.parts) % s.ny, place // len(s.parts) // s.ny
                rows = ins[place].reshape(s.nx * s.yc * ROWS, LANES)
                taken = rows[pl.ds(x, s.nx * s.yc, stride=ROWS), :]
                for r in range(s.nx):
                    at = from_ref[k] * s.b + px_ref[r] * s.by + chunk * s.yc
                    lines[pl.ds(pl.multiple_of(at, s.yc), s.yc), lanes] = taken[r * s.yc : (r + 1) * s.yc]
            moved[...] = times_lines((high_ref, low_ref), lines[...])
            for k in range(s.ny):
                outs[k][x] = moved[pl.ds(pl.multiple_of(to_ref[k] * s.b, s.b), s.b), :]

    turned = [
        pl.BlockSpec((s.nx, s.yc, ROWS, LANES), functools.partial(lambda part, i: (0, 0, i, part), part))
        for part, _ in s.parts
    ]
    plain = pl.BlockSpec((ROWS, s.b, s.c), lambda i: (i, 0, 0))
    return call(
        kernel,
        "y_lines_unturned",
        (s.ax // ROWS,),
        [table_spec()] * 3 + [whole_spec((s.full, s.full))] * 2 + turned * (s.chunks * s.ny),
        [plain] * s.ny,
        [jax.ShapeDtypeStruct((s.ax, s.b, s.c), F32)] * s.ny,
        [pltpu.VMEM((s.full, s.c), F32), pltpu.VMEM((s.full, s.c), F32)],
        6 * s.a * s.b * s.c * s.full,
        2 * s.field_bytes,
    )(from_px, from_py, to_py, *matrix, *[block for chunk in got for block in chunk for _ in s.parts])


def y_lines_turned(s, got, matrix, to_px, from_py, to_py):
    def kernel(px_ref, from_ref, to_ref, high_ref, low_ref, *rest):
        ins, outs = rest[: s.ny], rest[s.ny : -3]
        lines, moved, held = rest[-3:]

        @pl.loop(0, ROWS)
        def _(x):
            for k in range(s.ny):
                lines[pl.ds(pl.multiple_of(from_ref[k] * s.b, s.b), s.b), :] = ins[k][x]
            moved[...] = times_lines((high_ref, low_ref), lines[...])
            for chunk in range(s.chunks):
                for k in range(s.ny):
                    for r in range(s.nx):
                        at = to_ref[k] * s.b + px_ref[r] * s.by + chunk * s.yc
                        taken = moved[pl.ds(pl.multiple_of(at, s.yc), s.yc), :]
                        for part, lanes in s.parts:
                            place = pl.ds(x + r * s.yc * ROWS, s.yc, stride=ROWS)
                            held[part, chunk * s.ny + k, place, :] = taken[:, lanes]

        for place, out in enumerate(outs):
            for part, lanes in s.parts:
                out[:, :, :, lanes] = held[part, place].reshape(s.nx, s.yc, ROWS, LANES)

    turned = pl.BlockSpec((s.nx, s.yc, ROWS, s.c), lambda i: (0, 0, i, 0))
    plain = pl.BlockSpec((ROWS, s.b, s.c), lambda i: (i, 0, 0))
    outs = call(
        kernel,
        "y_lines_turned",
        (s.ax // ROWS,),
        [table_spec()] * 3 + [whole_spec((s.full, s.full))] * 2 + [plain] * s.ny,
        [turned] * (s.chunks * s.ny),
        [jax.ShapeDtypeStruct((s.nx, s.yc, s.ax, s.c), F32)] * (s.chunks * s.ny),
        [
            pltpu.VMEM((s.full, s.c), F32),
            pltpu.VMEM((s.full, s.c), F32),
            pltpu.VMEM((len(s.parts), s.chunks * s.ny, s.nx * s.yc * ROWS, LANES), F32),
        ],
        6 * s.a * s.b * s.c * s.full,
        2 * s.field_bytes,
    )(to_px, from_py, to_py, *matrix, *got)
    return [outs[chunk * s.ny : (chunk + 1) * s.ny] for chunk in range(s.chunks)]


def finish_forward(s, got, potential, end_adjoint, from_py):
    step = ROWS // 2

    def kernel(from_ref, w_ref, e_ref, *rest):
        ins, (final_ref, term_ref) = rest[: s.ny], rest[s.ny :]
        for k in range(s.ny):
            q = from_ref[k]
            final = half_of(w_ref[q]) * ins[k][...]
            final_ref[q] = final
            term_ref[q] = 0.05 * final * e_ref[q]

    block = pl.BlockSpec((s.ny, step, s.b, s.c), lambda i: (0, i, 0, 0))
    plain = pl.BlockSpec((step, s.b, s.c), lambda i: (i, 0, 0))
    view = (s.ny, s.ax, s.b, s.c)
    outs = call(
        kernel,
        "finish_forward",
        (s.ax // step,),
        [table_spec(), block, block] + [plain] * s.ny,
        [block, block],
        [jax.ShapeDtypeStruct(view, F32)] * 2,
        [],
        s.a * s.b * s.c * 4,
        5 * s.field_bytes,
    )(from_py, potential.reshape(view), end_adjoint.reshape(view), *got)
    return [out.reshape(s.a, s.b, s.c) for out in outs]


def finish_adjoint(s, got, chunk, potential, start_field, density, first, from_px):
    def kernel(from_ref, w_ref, f_ref, term_ref, *rest):
        ins, (first_ref, density_ref) = rest[: s.nx], rest[-2:]
        for r in range(s.nx):
            p = from_ref[r]
            value = half_of(w_ref[:, p]) * ins[r][...]
            first_ref[:, p] = value
            density_ref[:, p] = term_ref[:, p] + 0.05 * f_ref[:, p] * value

    view = (s.a, s.nx, s.by, s.c)
    block = pl.BlockSpec((2 * ROWS, s.nx, s.yc, s.c), lambda i: (i, 0, chunk, 0))
    plain = pl.BlockSpec((2 * ROWS, s.yc, s.c), lambda i: (i, 0, 0))
    outs = call(
        kernel,
        "finish_adjoint",
        (s.a // (2 * ROWS),),
        [table_spec(), block, block, block] + [plain] * s.nx,
        [block, block],
        [jax.ShapeDtypeStruct(view, F32)] * 2,
        [],
        s.a * s.b * s.c * 4 // s.chunks,
        6 * s.field_bytes // s.chunks,
        {3: 1},
    )(from_px, potential.reshape(view), start_field.reshape(view), density.reshape(view), *got)
    return [out.reshape(s.a, s.b, s.c) for out in outs]


def finish_block(s, got, chunk, potential, start_field, density, first, source):
    def kernel(source_ref, got_ref, w_ref, f_ref, term_ref, whole_ref, first_ref, density_ref):
        value = half_of(w_ref[...]) * got_ref[...].reshape(w_ref.shape)
        first_ref[...] = value
        density_ref[...] = term_ref[...] + 0.05 * f_ref[...] * value

    step = s.a // 2
    view = (s.a, s.nx, s.by, s.c)
    block = pl.BlockSpec((step, 1, s.yc, s.c), lambda i, source_ref: (i, source_ref[0], chunk, 0))
    touched = 6 * s.field_bytes // s.chunks // s.nx
    outs = pl.pallas_call(
        kernel,
        name="finish_block",
        grid_spec=pltpu.PrefetchScalarGridSpec(
            num_scalar_prefetch=1,
            grid=(s.a // step,),
            in_specs=[pl.BlockSpec((step, s.yc, s.c), lambda i, source_ref: (i, 0, 0))]
            + [block] * 3
            + [pl.BlockSpec(memory_space=pl.ANY)],
            out_specs=[block, block],
        ),
        out_shape=[jax.ShapeDtypeStruct(view, F32)] * 2,
        input_output_aliases={4: 1, 5: 0},
        cost_estimate=pl.CostEstimate(flops=0, bytes_accessed=touched, transcendentals=0),
        compiler_params=pltpu.CompilerParams(vmem_limit_bytes=VMEM_LIMIT),
    )(source, got, *(array.reshape(view) for array in (potential, start_field, density, first)))
    return [out.reshape(s.a, s.b, s.c) for out in outs]


def gather(s, blocks, count):
    return [jnp.stack([block[r] for block in blocks]) for r in range(count)]


def tiled_body(s, start_field, end_adjoint, potential, line_xy, line_z):
    me_px, me_py = lax.axis_index("px"), lax.axis_index("py")
    to_px, from_px = (f(me_px, jnp.arange(s.nx, dtype=jnp.int32), s.nx) for f in (to_of, from_of))
    to_py, from_py = (f(me_py, jnp.arange(s.ny, dtype=jnp.int32), s.ny) for f in (to_of, from_of))
    xy, xy_turned, z, z_turned = (two_parts(m) for m in (line_xy, line_xy.T, line_z, line_z.T))

    flow = Flow({"px": 4, "py": 3}, {"work": 4, "py": 12})
    px, py = functools.partial(Exchange, flow, "px"), functools.partial(Exchange, flow, "py")
    last = s.chunks - 1

    f_in = [px(flow.work(first_in, s, start_field, 0, potential, z_turned, to_px)).send(2)]
    for chunk in range(1, s.chunks):
        f_in.append(px(flow.work(first_in, s, start_field, chunk, potential, z_turned, to_px)))
    f_in[0].send(3)
    a_in = py(flow.work(first_by_py, s, end_adjoint, potential, z, to_py))
    a_in.send(1)
    f_in[0].rest()
    for chunk in range(1, s.chunks):
        f_in[chunk].send(1)
        a_in.send(1)
        f_in[chunk].send(1)
    f_out = [px(flow.work(x_lines_forward, s, f_in[0].rest(), xy, from_px, to_px, to_py))]
    f_in[last].send(2)
    adjoint = a_in.rest()
    for stage in f_in:
        stage.rest()
    f_out[0].send(4)
    for chunk in range(1, s.chunks):
        f_out.append(px(flow.work(x_lines_forward, s, f_in[chunk].rest(), xy, from_px, to_px, to_py)))
    adjoint = flow.work(y_lines_turned, s, adjoint, xy_turned, to_px, from_py, to_py)
    a_back = [py(blocks) for blocks in adjoint]

    for chunk in range(s.chunks):
        a_back[chunk].send(1)
        f_out[chunk].send(1)
        a_back[chunk].send(1)
        f_out[chunk].send(2)
        a_back[chunk].send(1)
        if chunk < last:
            f_out[chunk].rest()
    f_out[last].send(1)
    a_in = [px(flow.work(gather, s, a_back[0].rest(), s.nx))]
    f_in = [py(flow.work(gather, s, f_out[0].got, s.ny))]
    f_in[0].send(1)
    f_out[last].send(2)
    f_in[0].send(1)
    for chunk in range(1, s.chunks):
        a_in.append(px(flow.work(gather, s, a_back[chunk].rest(), s.nx)))
    f_out[last].rest()
    f_in[0].send(1)
    a_in[0].send(3)

    for chunk in range(1, s.chunks):
        f_in.append(py(flow.work(gather, s, f_out[chunk].got, s.ny)))
    f_in[last].send(1)
    a_in[0].send(2)
    f_in[last].send(1)
    a_in[0].rest()
    f_in[last].rest()
    a_in[last].send(3)
    forward = [stage.rest() for stage in f_in]
    f_back = py(flow.work(y_lines_unturned, s, forward, xy, from_px, from_py, to_py))
    a_out = [px(flow.work(x_lines_adjoint, s, a_in[0].rest(), xy_turned, from_px, to_px, from_py))]
    a_in[last].send(2)
    f_back.send(1)
    for stage in a_in:
        stage.rest()
    a_out[0].send(2)
    f_back.send(1)
    a_out[0].send(2)
    f_back.rest()
    for chunk in range(1, s.chunks):
        a_out.append(px(flow.work(x_lines_adjoint, s, a_in[chunk].rest(), xy_turned, from_px, to_px, from_py)))
    a_out[0].send(3)
    final, density = flow.work(finish_forward, s, f_back.rest(), potential, end_adjoint, from_py, back=False)
    a_out[0].rest()
    a_out[last].send(3)
    args = (0, potential, start_field, density, None, from_px)
    first, density = flow.work(finish_adjoint, s, a_out[0].rest(), *args, back=False)
    for chunk in range(1, s.chunks):
        a_out[chunk].send(len(a_out[chunk].left) - 3)
        flow.settle(4)
        a_out[chunk].rest()
        for r in [0, *a_out[chunk].order]:
            args = (chunk, potential, start_field, density, first, from_px[r : r + 1])
            first, density = finish_block(s, a_out[chunk].got[r], *args)
    return final, first, density


def plain_body(s, start_field, end_adjoint, potential, line_xy, line_z):
    half = half_of(potential)

    def step(field, matrix_xy, matrix_z):
        lines = product(half * field, matrix_z.T)
        lines = lax.all_to_all(lines, "px", 1, 0, tiled=True)
        lines = product(matrix_xy, lines.reshape(s.full, -1)).reshape(lines.shape)
        lines = lax.all_to_all(lines, "px", 0, 1, tiled=True)
        lines = lax.all_to_all(lines, "py", 0, 1, tiled=True)
        lines = jnp.einsum("ij,ajc->aic", matrix_xy, lines, precision=lax.Precision.HIGHEST)
        return half * lax.all_to_all(lines, "py", 1, 0, tiled=True)

    final = step(start_field, line_xy, line_z)
    first = step(end_adjoint, line_xy.T, line_z.T)
    return final, first, 0.05 * start_field * first + 0.05 * final * end_adjoint


def body(start_field, end_adjoint, potential, line_xy, line_z):
    s = Sizes(start_field.shape, lax.axis_size("px"), lax.axis_size("py"))
    even = s.nx % 2 == 0 and s.ny % 2 == 0
    whole_tiles = s.by % ROWS == 0 and s.ax % ROWS == 0 and s.c % 128 == 0
    run = tiled_body if even and whole_tiles and s.by and s.ax else plain_body
    return run(s, start_field, end_adjoint, potential, line_xy, line_z)


def solution(mesh):
    placed = (P("px", "py", None), P("px", "py", None), P("px", "py", None), P(), P())
    return jax.shard_map(
        body,
        mesh=mesh,
        in_specs=placed,
        out_specs=(P("px", "py", None), P("px", "py", None), P("px", "py", None)),
        check_vma=False,
    )
```

```python
import functools

import jax
import jax.numpy as jnp
from jax import lax
from jax.experimental import pallas as pl
from jax.experimental.pallas import tpu as pltpu
from jax.sharding import PartitionSpec as P

F32 = jnp.float32
ROWS = 8
LANES = 128
VMEM_LIMIT = 56 * 1024 * 1024


def product(left, right):
    return jnp.dot(left, right, precision=lax.Precision.HIGHEST, preferred_element_type=F32)


def two_parts(value):
    high = lax.reduce_precision(value, 8, 7)
    return [high.astype(jnp.bfloat16), (value - high).astype(jnp.bfloat16)]


def split_in_kernel(value):
    high = value.astype(jnp.bfloat16)
    return high, (value - high.astype(F32)).astype(jnp.bfloat16)


def dot(left, right):
    return jnp.dot(left, right, preferred_element_type=F32)


def lines_times(lines, matrix_refs):
    high, low = split_in_kernel(lines)
    matrix_high, matrix_low = matrix_refs[0][...], matrix_refs[1][...]
    return dot(high, matrix_high) + (dot(high, matrix_low) + dot(low, matrix_high))


def times_lines(matrix_refs, lines):
    high, low = split_in_kernel(lines)
    matrix_high, matrix_low = matrix_refs[0][...], matrix_refs[1][...]
    return dot(matrix_high, high) + (dot(matrix_low, high) + dot(matrix_high, low))


def half_of(potential):
    return jnp.exp(-0.05 * potential)


def call(kernel, name, grid, in_specs, out_specs, outs, scratch, flops, touched, aliases=None):
    return pl.pallas_call(
        kernel,
        name=name,
        grid=grid,
        in_specs=in_specs,
        out_specs=out_specs,
        out_shape=outs,
        scratch_shapes=scratch,
        input_output_aliases=aliases or {},
        cost_estimate=pl.CostEstimate(flops=flops, bytes_accessed=touched, transcendentals=0),
        compiler_params=pltpu.CompilerParams(vmem_limit_bytes=VMEM_LIMIT),
    )


def table_spec():
    return pl.BlockSpec(memory_space=pltpu.SMEM)


def whole_spec(shape):
    return pl.BlockSpec(shape, lambda i: (0,) * len(shape))


def to_of(me, r, n):
    pairs = n // 2
    return ((me // 2 + r // 2) % pairs) * 2 + (me % 2 + r % 2) % 2


def from_of(me, r, n):
    pairs = n // 2
    return ((me // 2 + pairs - r // 2) % pairs) * 2 + (me % 2 + r % 2) % 2


def after(value, *earlier):
    if isinstance(value, list):
        return [after(value[0], *earlier), *value[1:]]
    return lax.optimization_barrier((value, *earlier))[0] if earlier else value


class Flow:
    def __init__(self, depth, lag):
        self.depth, self.lag = depth, lag
        self.landed = {"px": [], "py": []}
        self.latest = []
        self.due = []

    def back(self, axis):
        landed, depth = self.landed[axis], self.depth[axis]
        return landed[max(0, len(landed) - 2 * depth + 1) : max(0, len(landed) - depth + 1)]

    def owe(self, kind, array):
        self.due.append((len(self.landed["px"]) + self.lag[kind], array))

    def work(self, function, s, value, *rest, back=True):
        out = function(s, after(value, *self.latest, *(self.back("px") if back else [])), *rest)
        self.latest = [jax.tree.leaves(out)[0]]
        self.owe("work", self.latest[0])
        return out

    def settle(self, depth):
        self.due = [(0, array) for _, array in self.due]
        self.depth["px"] = depth

    def permute(self, axis, block, pairs):
        count = len(self.landed["px"])
        if axis == "px":
            pins = self.back("px") + [array for when, array in self.due if when <= count]
            self.due = [(when, array) for when, array in self.due if when > count]
        else:
            pins = self.back("py") + self.back("px")[-1:]
        got = lax.ppermute(after(block, *pins), axis, pairs)
        self.landed[axis].append(got)
        if axis == "py":
            self.owe("py", got)
        return got


class Exchange:
    def __init__(self, flow, axis, blocks):
        self.flow, self.axis, self.blocks, self.n = flow, axis, blocks, len(blocks)
        self.got = [blocks[0]] + [None] * (self.n - 1)
        self.order = sorted(range(1, self.n), key=lambda r: (r % 2, abs(2 * (r // 2) - self.n // 2), r))
        self.left = list(self.order)

    def send(self, count):
        for r in self.left[:count]:
            pairs = [(device, to_of(device, r, self.n)) for device in range(self.n)]
            self.got[r] = self.flow.permute(self.axis, self.blocks[r], pairs)
        self.left = self.left[count:]
        return self

    def rest(self):
        return self.send(self.n).got


class Sizes:
    def __init__(self, field_shape, count_px, count_py):
        self.nx, self.ny = count_px, count_py
        self.a, self.b, self.c = field_shape
        self.full = self.a * count_px
        self.by = self.b // count_px
        self.ax = self.a // count_py
        self.yc = ROWS
        self.chunks = self.by // ROWS
        self.parts = [(k, slice(k * LANES, (k + 1) * LANES)) for k in range(self.c // LANES)]
        self.field_bytes = 4 * self.a * self.b * self.c


def turn_spec(s, part):
    return pl.BlockSpec((s.a, s.yc, LANES), lambda i: (0, 0, part))


def first_in(s, field, chunk, potential, z_turned, to_px):
    def kernel(to_ref, f_ref, w_ref, high_ref, low_ref, *rest):
        outs, held = rest[:-1], rest[-1]
        moved = half_of(w_ref[...]) * f_ref[...]
        moved = lines_times(moved.reshape(2 * ROWS * s.nx * s.yc, s.c), (high_ref, low_ref))
        held[...] = moved.reshape(2 * ROWS, s.nx, s.yc, s.c)
        for r, out in enumerate(outs):
            out[...] = held[:, to_ref[r]]

    block = pl.BlockSpec((2 * ROWS, s.nx, s.yc, s.c), lambda i: (i, 0, chunk, 0))
    out = pl.BlockSpec((2 * ROWS, s.yc, s.c), lambda i: (i, 0, 0))
    view = (s.a, s.nx, s.by, s.c)
    return call(
        kernel,
        "z_lines_by_px",
        (s.a // (2 * ROWS),),
        [table_spec(), block, block] + [whole_spec((s.c, s.c))] * 2,
        [out] * s.nx,
        [jax.ShapeDtypeStruct((s.a, s.yc, s.c), F32)] * s.nx,
        [pltpu.VMEM((2 * ROWS, s.nx, s.yc, s.c), F32)],
        6 * s.a * s.b * s.c * s.c // s.chunks,
        3 * s.field_bytes // s.chunks,
    )(to_px, field.reshape(view), potential.reshape(view), *z_turned)


def first_by_py(s, field, potential, z_turned, to_py):
    step = ROWS // 2

    def kernel(to_ref, f_ref, w_ref, high_ref, low_ref, *outs):
        for r in range(s.ny):
            q = to_ref[r]
            moved = half_of(w_ref[q]) * f_ref[q]
            moved = lines_times(moved.reshape(step * s.b, s.c), (high_ref, low_ref))
            outs[r][...] = moved.reshape(step, s.b, s.c)

    block = pl.BlockSpec((s.ny, step, s.b, s.c), lambda i: (0, i, 0, 0))
    out = pl.BlockSpec((step, s.b, s.c), lambda i: (i, 0, 0))
    view = (s.ny, s.ax, s.b, s.c)
    return call(
        kernel,
        "z_lines_by_py",
        (s.ax // step,),
        [table_spec(), block, block] + [whole_spec((s.c, s.c))] * 2,
        [out] * s.ny,
        [jax.ShapeDtypeStruct((s.ax, s.b, s.c), F32)] * s.ny,
        [],
        6 * s.a * s.b * s.c * s.c,
        3 * s.field_bytes,
    )(to_py, field.reshape(view), potential.reshape(view), *z_turned)


def x_lines_forward(s, got, matrix, from_px, to_px, to_py):
    def kernel(from_ref, to_ref, part_ref, high_ref, low_ref, *rest):
        count = len(s.parts) * s.nx
        ins, outs = rest[:count], rest[count:-2]
        lines, moved = rest[-2:]
        y = pl.program_id(0)
        for place in range(count):
            r, (_, lanes) = place // len(s.parts), s.parts[place % len(s.parts)]
            rows = ins[place].reshape(s.a * s.yc, LANES)
            lines[pl.ds(pl.multiple_of(from_ref[r] * s.a, s.a), s.a), lanes] = rows[pl.ds(y, s.a, stride=s.yc), :]
        moved[...] = times_lines((high_ref, low_ref), lines[...])
        for r in range(s.nx):
            for k in range(s.ny):
                at = pl.multiple_of(to_ref[r] * s.a + part_ref[k] * s.ax, s.ax)
                outs[r][k, 0] = moved[pl.ds(at, s.ax), :]

    parted = pl.BlockSpec((s.ny, 1, s.ax, s.c), lambda i: (0, i, 0, 0))
    return call(
        kernel,
        "x_lines_forward",
        (s.yc,),
        [table_spec()] * 3
        + [whole_spec((s.full, s.full))] * 2
        + [turn_spec(s, part) for _ in range(s.nx) for part, _ in s.parts],
        [parted] * s.nx,
        [jax.ShapeDtypeStruct((s.ny, s.yc, s.ax, s.c), F32)] * s.nx,
        [pltpu.VMEM((s.full, s.c), F32), pltpu.VMEM((s.full, s.c), F32)],
        6 * s.a * s.b * s.c * s.full // s.chunks,
        2 * s.field_bytes // s.chunks,
    )(from_px, to_px, to_py, *matrix, *[block for block in got for _ in s.parts])


def x_lines_adjoint(s, got, matrix, from_px, to_px, from_py):
    def kernel(from_ref, to_ref, part_ref, high_ref, low_ref, *rest):
        ins, outs = rest[: s.nx], rest[s.nx : -3]
        lines, moved, held = rest[-3:]
        y = pl.program_id(0)
        for r in range(s.nx):
            for k in range(s.ny):
                at = pl.multiple_of(from_ref[r] * s.a + part_ref[k] * s.ax, s.ax)
                lines[pl.ds(at, s.ax), :] = ins[r][k, 0]
        moved[...] = times_lines((high_ref, low_ref), lines[...])
        for r in range(s.nx):
            for part, lanes in s.parts:
                taken = moved[pl.ds(pl.multiple_of(to_ref[r] * s.a, s.a), s.a), lanes]
                held[part, r, pl.ds(y, s.a, stride=s.yc), :] = taken

        @pl.when(y == s.yc - 1)
        def _():
            for r in range(s.nx):
                for part, lanes in s.parts:
                    outs[r][:, :, lanes] = held[part, r].reshape(s.a, s.yc, LANES)

    parted = pl.BlockSpec((s.ny, 1, s.ax, s.c), lambda i: (0, i, 0, 0))
    return call(
        kernel,
        "x_lines_adjoint",
        (s.yc,),
        [table_spec()] * 3 + [whole_spec((s.full, s.full))] * 2 + [parted] * s.nx,
        [whole_spec((s.a, s.yc, s.c))] * s.nx,
        [jax.ShapeDtypeStruct((s.a, s.yc, s.c), F32)] * s.nx,
        [
            pltpu.VMEM((s.full, s.c), F32),
            pltpu.VMEM((s.full, s.c), F32),
            pltpu.VMEM((len(s.parts), s.nx, s.a * s.yc, LANES), F32),
        ],
        6 * s.a * s.b * s.c * s.full // s.chunks,
        2 * s.field_bytes // s.chunks,
    )(from_px, to_px, from_py, *matrix, *got)


def y_lines_unturned(s, got, matrix, from_px, from_py, to_py):
    def kernel(px_ref, from_ref, to_ref, high_ref, low_ref, *rest):
        count = len(s.parts) * s.chunks * s.ny
        ins, outs = rest[:count], rest[count:-2]
        lines, moved = rest[-2:]

        @pl.loop(0, ROWS)
        def _(x):
            for place in range(count):
                part, lanes = s.parts[place % len(s.parts)]
                k, chunk = place // len(s.parts) % s.ny, place // len(s.parts) // s.ny
                rows = ins[place].reshape(s.nx * s.yc * ROWS, LANES)
                taken = rows[pl.ds(x, s.nx * s.yc, stride=ROWS), :]
                for r in range(s.nx):
                    at = from_ref[k] * s.b + px_ref[r] * s.by + chunk * s.yc
                    lines[pl.ds(pl.multiple_of(at, s.yc), s.yc), lanes] = taken[r * s.yc : (r + 1) * s.yc]
            moved[...] = times_lines((high_ref, low_ref), lines[...])
            for k in range(s.ny):
                outs[k][x] = moved[pl.ds(pl.multiple_of(to_ref[k] * s.b, s.b), s.b), :]

    turned = [
        pl.BlockSpec((s.nx, s.yc, ROWS, LANES), functools.partial(lambda part, i: (0, 0, i, part), part))
        for part, _ in s.parts
    ]
    plain = pl.BlockSpec((ROWS, s.b, s.c), lambda i: (i, 0, 0))
    return call(
        kernel,
        "y_lines_unturned",
        (s.ax // ROWS,),
        [table_spec()] * 3 + [whole_spec((s.full, s.full))] * 2 + turned * (s.chunks * s.ny),
        [plain] * s.ny,
        [jax.ShapeDtypeStruct((s.ax, s.b, s.c), F32)] * s.ny,
        [pltpu.VMEM((s.full, s.c), F32), pltpu.VMEM((s.full, s.c), F32)],
        6 * s.a * s.b * s.c * s.full,
        2 * s.field_bytes,
    )(from_px, from_py, to_py, *matrix, *[block for chunk in got for block in chunk for _ in s.parts])


def y_lines_turned(s, got, matrix, to_px, from_py, to_py):
    def kernel(px_ref, from_ref, to_ref, high_ref, low_ref, *rest):
        ins, outs = rest[: s.ny], rest[s.ny : -3]
        lines, moved, held = rest[-3:]

        @pl.loop(0, ROWS)
        def _(x):
            for k in range(s.ny):
                lines[pl.ds(pl.multiple_of(from_ref[k] * s.b, s.b), s.b), :] = ins[k][x]
            moved[...] = times_lines((high_ref, low_ref), lines[...])
            for chunk in range(s.chunks):
                for k in range(s.ny):
                    for r in range(s.nx):
                        at = to_ref[k] * s.b + px_ref[r] * s.by + chunk * s.yc
                        taken = moved[pl.ds(pl.multiple_of(at, s.yc), s.yc), :]
                        for part, lanes in s.parts:
                            place = pl.ds(x + r * s.yc * ROWS, s.yc, stride=ROWS)
                            held[part, chunk * s.ny + k, place, :] = taken[:, lanes]

        for place, out in enumerate(outs):
            for part, lanes in s.parts:
                out[:, :, :, lanes] = held[part, place].reshape(s.nx, s.yc, ROWS, LANES)

    turned = pl.BlockSpec((s.nx, s.yc, ROWS, s.c), lambda i: (0, 0, i, 0))
    plain = pl.BlockSpec((ROWS, s.b, s.c), lambda i: (i, 0, 0))
    outs = call(
        kernel,
        "y_lines_turned",
        (s.ax // ROWS,),
        [table_spec()] * 3 + [whole_spec((s.full, s.full))] * 2 + [plain] * s.ny,
        [turned] * (s.chunks * s.ny),
        [jax.ShapeDtypeStruct((s.nx, s.yc, s.ax, s.c), F32)] * (s.chunks * s.ny),
        [
            pltpu.VMEM((s.full, s.c), F32),
            pltpu.VMEM((s.full, s.c), F32),
            pltpu.VMEM((len(s.parts), s.chunks * s.ny, s.nx * s.yc * ROWS, LANES), F32),
        ],
        6 * s.a * s.b * s.c * s.full,
        2 * s.field_bytes,
    )(to_px, from_py, to_py, *matrix, *got)
    return [outs[chunk * s.ny : (chunk + 1) * s.ny] for chunk in range(s.chunks)]


def finish_forward(s, got, potential, end_adjoint, from_py):
    step = ROWS // 2

    def kernel(from_ref, w_ref, e_ref, *rest):
        ins, (final_ref, term_ref) = rest[: s.ny], rest[s.ny :]
        for k in range(s.ny):
            q = from_ref[k]
            final = half_of(w_ref[q]) * ins[k][...]
            final_ref[q] = final
            term_ref[q] = 0.05 * final * e_ref[q]

    block = pl.BlockSpec((s.ny, step, s.b, s.c), lambda i: (0, i, 0, 0))
    plain = pl.BlockSpec((step, s.b, s.c), lambda i: (i, 0, 0))
    view = (s.ny, s.ax, s.b, s.c)
    outs = call(
        kernel,
        "finish_forward",
        (s.ax // step,),
        [table_spec(), block, block] + [plain] * s.ny,
        [block, block],
        [jax.ShapeDtypeStruct(view, F32)] * 2,
        [],
        s.a * s.b * s.c * 4,
        5 * s.field_bytes,
    )(from_py, potential.reshape(view), end_adjoint.reshape(view), *got)
    return [out.reshape(s.a, s.b, s.c) for out in outs]


def finish_adjoint(s, got, chunk, potential, start_field, density, first, from_px):
    def kernel(from_ref, w_ref, f_ref, term_ref, *rest):
        ins, (first_ref, density_ref) = rest[: s.nx], rest[-2:]
        for r in range(s.nx):
            p = from_ref[r]
            value = half_of(w_ref[:, p]) * ins[r][...]
            first_ref[:, p] = value
            density_ref[:, p] = term_ref[:, p] + 0.05 * f_ref[:, p] * value

    view = (s.a, s.nx, s.by, s.c)
    block = pl.BlockSpec((2 * ROWS, s.nx, s.yc, s.c), lambda i: (i, 0, chunk, 0))
    plain = pl.BlockSpec((2 * ROWS, s.yc, s.c), lambda i: (i, 0, 0))
    outs = call(
        kernel,
        "finish_adjoint",
        (s.a // (2 * ROWS),),
        [table_spec(), block, block, block] + [plain] * s.nx,
        [block, block],
        [jax.ShapeDtypeStruct(view, F32)] * 2,
        [],
        s.a * s.b * s.c * 4 // s.chunks,
        6 * s.field_bytes // s.chunks,
        {3: 1},
    )(from_px, potential.reshape(view), start_field.reshape(view), density.reshape(view), *got)
    return [out.reshape(s.a, s.b, s.c) for out in outs]


def finish_block(s, got, chunk, potential, start_field, density, first, source):
    def kernel(source_ref, got_ref, w_ref, f_ref, term_ref, whole_ref, first_ref, density_ref):
        value = half_of(w_ref[...]) * got_ref[...].reshape(w_ref.shape)
        first_ref[...] = value
        density_ref[...] = term_ref[...] + 0.05 * f_ref[...] * value

    step = s.a
    view = (s.a, s.nx, s.by, s.c)
    block = pl.BlockSpec((step, 1, s.yc, s.c), lambda i, source_ref: (i, source_ref[0], chunk, 0))
    touched = 6 * s.field_bytes // s.chunks // s.nx
    outs = pl.pallas_call(
        kernel,
        name="finish_block",
        grid_spec=pltpu.PrefetchScalarGridSpec(
            num_scalar_prefetch=1,
            grid=(s.a // step,),
            in_specs=[pl.BlockSpec((step, s.yc, s.c), lambda i, source_ref: (i, 0, 0))]
            + [block] * 3
            + [pl.BlockSpec(memory_space=pl.ANY)],
            out_specs=[block, block],
        ),
        out_shape=[jax.ShapeDtypeStruct(view, F32)] * 2,
        input_output_aliases={4: 1, 5: 0},
        cost_estimate=pl.CostEstimate(flops=0, bytes_accessed=touched, transcendentals=0),
        compiler_params=pltpu.CompilerParams(vmem_limit_bytes=VMEM_LIMIT),
    )(source, got, *(array.reshape(view) for array in (potential, start_field, density, first)))
    return [out.reshape(s.a, s.b, s.c) for out in outs]


def gather(s, blocks, count):
    return [jnp.stack([block[r] for block in blocks]) for r in range(count)]


def tiled_body(s, start_field, end_adjoint, potential, line_xy, line_z):
    me_px, me_py = lax.axis_index("px"), lax.axis_index("py")
    to_px, from_px = (f(me_px, jnp.arange(s.nx, dtype=jnp.int32), s.nx) for f in (to_of, from_of))
    to_py, from_py = (f(me_py, jnp.arange(s.ny, dtype=jnp.int32), s.ny) for f in (to_of, from_of))
    xy, xy_turned, z, z_turned = (two_parts(m) for m in (line_xy, line_xy.T, line_z, line_z.T))

    flow = Flow({"px": 4, "py": 3}, {"work": 4, "py": 12})
    px, py = functools.partial(Exchange, flow, "px"), functools.partial(Exchange, flow, "py")
    last = s.chunks - 1

    f_in = [px(flow.work(first_in, s, start_field, 0, potential, z_turned, to_px)).send(2)]
    for chunk in range(1, s.chunks):
        f_in.append(px(flow.work(first_in, s, start_field, chunk, potential, z_turned, to_px)))
    f_in[0].send(3)
    a_in = py(flow.work(first_by_py, s, end_adjoint, potential, z, to_py))
    a_in.send(1)
    f_in[0].rest()
    for chunk in range(1, s.chunks):
        f_in[chunk].send(1)
        a_in.send(1)
        f_in[chunk].send(1)
    f_out = [px(flow.work(x_lines_forward, s, f_in[0].rest(), xy, from_px, to_px, to_py))]
    f_in[last].send(2)
    adjoint = a_in.rest()
    for stage in f_in:
        stage.rest()
    f_out[0].send(4)
    for chunk in range(1, s.chunks):
        f_out.append(px(flow.work(x_lines_forward, s, f_in[chunk].rest(), xy, from_px, to_px, to_py)))
    adjoint = flow.work(y_lines_turned, s, adjoint, xy_turned, to_px, from_py, to_py)
    a_back = [py(blocks) for blocks in adjoint]

    for chunk in range(s.chunks):
        a_back[chunk].send(1)
        f_out[chunk].send(1)
        a_back[chunk].send(1)
        f_out[chunk].send(2)
        a_back[chunk].send(1)
        if chunk < last:
            f_out[chunk].rest()
    f_out[last].send(1)
    a_in = [px(flow.work(gather, s, a_back[0].rest(), s.nx))]
    f_in = [py(flow.work(gather, s, f_out[0].got, s.ny))]
    f_in[0].send(1)
    f_out[last].send(2)
    f_in[0].send(1)
    for chunk in range(1, s.chunks):
        a_in.append(px(flow.work(gather, s, a_back[chunk].rest(), s.nx)))
    f_out[last].rest()
    f_in[0].send(1)
    a_in[0].send(3)

    for chunk in range(1, s.chunks):
        f_in.append(py(flow.work(gather, s, f_out[chunk].got, s.ny)))
    f_in[last].send(1)
    a_in[0].send(2)
    f_in[last].send(1)
    a_in[0].rest()
    f_in[last].rest()
    a_in[last].send(3)
    forward = [stage.rest() for stage in f_in]
    f_back = py(flow.work(y_lines_unturned, s, forward, xy, from_px, from_py, to_py))
    a_out = [px(flow.work(x_lines_adjoint, s, a_in[0].rest(), xy_turned, from_px, to_px, from_py))]
    a_in[last].send(2)
    f_back.send(1)
    for stage in a_in:
        stage.rest()
    a_out[0].send(2)
    f_back.send(1)
    a_out[0].send(2)
    f_back.rest()
    for chunk in range(1, s.chunks):
        a_out.append(px(flow.work(x_lines_adjoint, s, a_in[chunk].rest(), xy_turned, from_px, to_px, from_py)))
    a_out[0].send(3)
    final, density = flow.work(finish_forward, s, f_back.rest(), potential, end_adjoint, from_py, back=False)
    a_out[0].rest()
    a_out[last].send(3)
    args = (0, potential, start_field, density, None, from_px)
    first, density = flow.work(finish_adjoint, s, a_out[0].rest(), *args, back=False)
    for chunk in range(1, s.chunks):
        flow.settle(4)
        a_out[chunk].rest()
        for r in [0, *a_out[chunk].order]:
            args = (chunk, potential, start_field, density, first, from_px[r : r + 1])
            first, density = finish_block(s, a_out[chunk].got[r], *args)
    return final, first, density


def plain_body(s, start_field, end_adjoint, potential, line_xy, line_z):
    half = half_of(potential)

    def step(field, matrix_xy, matrix_z):
        lines = product(half * field, matrix_z.T)
        lines = lax.all_to_all(lines, "px", 1, 0, tiled=True)
        lines = product(matrix_xy, lines.reshape(s.full, -1)).reshape(lines.shape)
        lines = lax.all_to_all(lines, "px", 0, 1, tiled=True)
        lines = lax.all_to_all(lines, "py", 0, 1, tiled=True)
        lines = jnp.einsum("ij,ajc->aic", matrix_xy, lines, precision=lax.Precision.HIGHEST)
        return half * lax.all_to_all(lines, "py", 1, 0, tiled=True)

    final = step(start_field, line_xy, line_z)
    first = step(end_adjoint, line_xy.T, line_z.T)
    return final, first, 0.05 * start_field * first + 0.05 * final * end_adjoint


def body(start_field, end_adjoint, potential, line_xy, line_z):
    s = Sizes(start_field.shape, lax.axis_size("px"), lax.axis_size("py"))
    even = s.nx % 2 == 0 and s.ny % 2 == 0
    whole_tiles = s.by % ROWS == 0 and s.ax % ROWS == 0 and s.c % 128 == 0
    run = tiled_body if even and whole_tiles and s.by and s.ax else plain_body
    return run(s, start_field, end_adjoint, potential, line_xy, line_z)


def solution(mesh):
    placed = (P("px", "py", None), P("px", "py", None), P("px", "py", None), P(), P())
    return jax.shard_map(
        body,
        mesh=mesh,
        in_specs=placed,
        out_specs=(P("px", "py", None), P("px", "py", None), P("px", "py", None)),
        check_vma=False,
    )
```
